32 devices in a mesh: dp: 8 (over z, y), ctx: 2 (over x), fsdp: 2 (over core).
Axes of the slice: x: 2, y: 2, z: 4, core: 2. Of those that a mesh axis runs over, the one named last changes fastest.
Arguments:
- layer_input: bfloat16 [16, 1024, 896], P(('dp', 'fsdp'), 'ctx'), may hold values from -6 to 6
- w_qkv: bfloat16 [896, 1152], P('fsdp'), may hold values from -0.1875 to 0.1875
- b_qkv: bfloat16 [1152], P('fsdp'), may hold values from -3 to 3
- g_attn: bfloat16 [896], P('fsdp'), may hold values from 0.25 to 1.75
- w_out: bfloat16 [896, 896], P('fsdp'), may hold values from -0.75 to 0.75
- g_mlp: bfloat16 [896], P('fsdp'), may hold values from 0.25 to 1.75
- w_gate: bfloat16 [896, 4864], P('fsdp'), may hold values from -0.1875 to 0.1875
- w_up: bfloat16 [896, 4864], P('fsdp'), may hold values from -0.1875 to 0.1875
- w_down: bfloat16 [4864, 896], P('fsdp'), may hold values from -0.078125 to 0.078125
- cotangent: bfloat16 [16, 1024, 896], P(('dp', 'fsdp'), 'ctx'), may hold values from -6 to 6
Outputs:
- activations: float32 [16, 1024, 896], P(('dp', 'fsdp'), 'ctx')
- grad_input: float32 [16, 1024, 896], P(('dp', 'fsdp'), 'ctx')
- grad_w_qkv: float32 [896, 1152], P('fsdp', ('dp', 'ctx'))
- grad_b_qkv: float32 [1152], P('fsdp')
- grad_g_attn: float32 [896], P('fsdp')
- grad_w_out: float32 [896, 896], P('fsdp', ('dp', 'ctx'))
- grad_g_mlp: float32 [896], P('fsdp')
- grad_w_gate: float32 [896, 4864], P('fsdp', ('dp', 'ctx'))
- grad_w_up: float32 [896, 4864], P('fsdp', ('dp', 'ctx'))
- grad_w_down: float32 [4864, 896], P('fsdp', ('dp', 'ctx'))
The draws below stay inside these ranges and needn't reach their ends.
All inputs are finite; a program needn't handle non-finite values.
Results may differ from the reference program's by a relative error of at most 0.015.
Values may be sent and summed in bfloat16 or wider, within the bound.
A program may use at most 192 MiB of HBM per device.

```python
import jax
import jax.numpy as jnp
from jax import lax

D = 896
HQ = 14
KVH = 2
HD = 64
FF = 4864
LEN = 1024
ATT = 896
QKV = 1152
GROUP = 7
BATCH = 16


def block_scale(key, shape, shards, low, largest):
    level = 1.0
    for axis_at, shards_of in shards:
        steps = jax.random.uniform(jax.random.fold_in(jax.random.fold_in(key, 6), axis_at), (shards_of,), jnp.float32, low / len(shards), largest / len(shards))
        level = level * jnp.repeat(jnp.exp(steps), shape[axis_at] // shards_of).reshape((-1,) + (1,) * (len(shape) - 1 - axis_at))
    return level


def noise(key, shape, width, limit, cuts=(), kind=jnp.bfloat16):
    array = jax.random.normal(key, shape, jnp.float32) * width
    if len(cuts) > 0:
        array = block_scale(key, shape, cuts, -0.22, 0.18) * array
    return jnp.clip(array, min=-limit, max=limit).astype(kind)


def setup_inputs(seed: int = 0) -> dict:
    key_of = jax.random.split(jax.random.key(seed), 11)
    layer_input = noise(key_of[0], (BATCH, LEN, D), 1.0, 6.0, ((0, 16), (1, 2)))
    w_qkv = noise(key_of[1], (D, QKV), D ** -0.5, 0.1875, ((0, 2),))
    b_qkv = noise(key_of[2], (QKV,), 0.5, 3.0, ((0, 2),))
    g_attn = jnp.clip(1.0 + 0.15 * jax.random.normal(key_of[3], (D,), jnp.float32), 0.25, 1.75).astype(jnp.bfloat16)
    w_out = noise(key_of[4], (ATT, D), (ATT // 16) ** -0.5, 0.75, ((0, 2),))
    g_mlp = jnp.clip(1.0 + 0.15 * jax.random.normal(key_of[5], (D,), jnp.float32), 0.25, 1.75).astype(jnp.bfloat16)
    w_gate = noise(key_of[6], (D, FF), D ** -0.5, 0.1875, ((0, 2),))
    w_up = noise(key_of[7], (D, FF), D ** -0.5, 0.1875, ((0, 2),))
    w_down = noise(key_of[8], (FF, D), FF ** -0.5, 0.078125, ((0, 2),))
    cotangent = noise(key_of[9], (BATCH, LEN, D), 1.0, 6.0, ((0, 16), (1, 2)))
    return {"layer_input": layer_input, "w_qkv": w_qkv, "b_qkv": b_qkv, "g_attn": g_attn, "w_out": w_out, "g_mlp": g_mlp, "w_gate": w_gate, "w_up": w_up, "w_down": w_down, "cotangent": cotangent}


epsilon = 1e-06
rope_base = 1000000.0
highest = lax.Precision.HIGHEST

@jax.custom_vjp
def low(v):
    return lax.optimization_barrier(v.astype(jnp.bfloat16)).astype(jnp.float32)

@jax.custom_vjp
def low_back(v):
    return v

def low_keep(v):
    return (low(v), None)

def low_pass(kept, grad):
    return (grad,)

def back_keep(v):
    return (v, None)

def back_low(kept, grad):
    return (low(grad),)
low.defvjp(low_keep, low_pass)
low_back.defvjp(back_keep, back_low)

def matmul(left, right):
    return jnp.dot(left, right, precision=highest, preferred_element_type=jnp.float32)

def normalize(tensor, gain):
    return tensor * lax.rsqrt(lax.optimization_barrier(jnp.mean(tensor * tensor, axis=-1, keepdims=True)) + epsilon) * gain

def tables(positions):
    frequency = rope_base ** (-(2.0 * jnp.arange(HD // 2, dtype=jnp.float32)) / HD)
    angles = positions[:, None] * frequency[None, :]
    cos_table = jnp.cos(angles)
    sin_table = jnp.sin(angles)
    return (jnp.concatenate([cos_table, cos_table], -1), jnp.concatenate([sin_table, sin_table], -1))

def rotate(heads_in, cos_table, sin_table):
    half_dim = HD // 2
    turned = jnp.concatenate([-heads_in[..., half_dim:], heads_in[..., :half_dim]], -1)
    return heads_in * cos_table[:, None, :] + turned * sin_table[:, None, :]

def layer(inputs, w_qkv, b_qkv, g_attn, w_out, g_mlp, w_gate, w_up, w_down):
    length = inputs.shape[0]
    key_width = KVH * HD
    normed_one = low(normalize(inputs, g_attn))
    joined = low_back(matmul(normed_one, w_qkv) + b_qkv)
    cos_table, sin_table = tables(jnp.arange(length, dtype=jnp.float32))
    queries = low(rotate(joined[:, :ATT].reshape(length, HQ, HD), cos_table, sin_table))
    queries = queries.reshape(length, KVH, GROUP, HD)
    rotated_keys = low(rotate(joined[:, ATT:ATT + key_width].reshape(length, KVH, HD), cos_table, sin_table))
    values = low(joined[:, ATT + key_width:].reshape(length, KVH, HD))
    scores = jnp.einsum('tgqd,ugd->gqtu', queries, rotated_keys, precision=highest) * HD ** (-0.5)
    scores = low_back(scores)
    visible = jnp.arange(length)[None, :] <= jnp.arange(length)[:, None]
    scores = jnp.where(visible, scores, -1e+30)
    probabilities = low(jax.nn.softmax(scores, axis=-1))
    mixed = jnp.einsum('gqtu,ugd->tgqd', probabilities, values, precision=highest).reshape(length, ATT)
    mixed = low_back(low(mixed))
    hidden = inputs + low_back(matmul(mixed, w_out))
    normed_two = low(normalize(hidden, g_mlp))
    gate_pre = low_back(matmul(normed_two, w_gate))
    up_value = low_back(matmul(normed_two, w_up))
    product = low(jax.nn.silu(gate_pre) * up_value)
    return hidden + matmul(product, w_down)

def reference(layer_input, w_qkv, b_qkv, g_attn, w_out, g_mlp, w_gate, w_up, w_down, cotangent):
    params = tuple((tensor.astype(jnp.float32) for tensor in (w_qkv, b_qkv, g_attn, w_out, g_mlp, w_gate, w_up, w_down)))

    def visit(totals, pair):
        seq_input, seq_cot = pair
        output, pull = jax.vjp(layer, seq_input.astype(jnp.float32), *params)
        grads = pull(seq_cot.astype(jnp.float32))
        totals = tuple((total + grad for total, grad in zip(totals, grads[1:])))
        return (totals, (output, grads[0]))
    zeros = tuple((jnp.zeros_like(tensor) for tensor in params))
    totals, (outputs, input_grads) = lax.scan(visit, zeros, (layer_input, cotangent))
    return (outputs, input_grads, totals[0], totals[1], totals[2], totals[3], totals[4], totals[5], totals[6], totals[7])
```

```python
import functools

import jax
import jax.numpy as jnp
from jax import lax
from jax.experimental import pallas as pl
from jax.experimental.pallas import tpu as pltpu
from jax.sharding import PartitionSpec as P

HQ = 14
KVH = 2
HD = 64
ATT = 896
QKV = 1152
GROUP = 7

epsilon = 1e-06
rope_base = 1000000.0
masked_score = -1e30
f32 = jnp.float32
bf16 = jnp.bfloat16


def dot_rows(left, right):
    return lax.dot_general(left, right, (((0,), (0,)), ((), ())), preferred_element_type=f32)


def dot_last(left, right):
    return lax.dot_general(left, right, (((1,), (1,)), ((), ())), preferred_element_type=f32)


def dot(left, right):
    return jnp.dot(left, right, preferred_element_type=f32)


def partner(value, axis, bit):
    return lax.ppermute(value, axis, [(i, i ^ (1 << bit)) for i in range(lax.axis_size(axis))])


def bits_of(axis):
    return lax.axis_size(axis).bit_length() - 1


class Halving:
    def __init__(self, blocks, order):
        self.inner = blocks.shape[1:]
        self.dp_bits = bits_of("dp")
        self.bits = self.dp_bits + bits_of("ctx")
        self.order = list(order)
        self.free = self.held = blocks.reshape((2,) * self.bits + self.inner)

    def step(self):
        if not self.order:
            return
        axis, bit = self.order.pop(0)
        dim = (self.dp_bits if axis == "dp" else self.bits) - 1 - bit
        mine = (lax.axis_index(axis) >> bit) & 1
        sent = lax.dynamic_slice_in_dim(self.free, 1 - mine, 1, dim)
        kept = lax.dynamic_slice_in_dim(self.held, mine, 1, dim)
        self.free = (kept.astype(f32) + partner(sent, axis, bit).astype(f32)).astype(bf16)
        self.held = self.free

    def finish(self):
        while self.order:
            self.step()
        return self.free.reshape(self.inner)


def after(arrays, sums):
    together = lax.optimization_barrier((tuple(arrays), tuple(one.held for one in sums)))
    for one, held in zip(sums, together[1]):
        one.held = held
    return together[0]


def step_all(sums):
    for one in sums:
        one.step()


def sum_everywhere(vector):
    for axis in ("fsdp", "ctx", "dp"):
        for bit in range(bits_of(axis)):
            vector = vector + partner(vector, axis, bit)
    return vector


def tables(positions, width):
    frequency = rope_base ** (-(2.0 * jnp.arange(HD // 2, dtype=f32)) / HD)
    angles = positions[:, None] * frequency[None, :]
    cos_table = jnp.tile(jnp.cos(angles), (1, width // (HD // 2)))
    sin_table = jnp.tile(jnp.sin(angles), (1, width // (HD // 2)))
    return cos_table, sin_table


def swap_halves(flat):
    half = HD // 2
    lower = (jnp.arange(flat.shape[1]) % HD < half)[None, :]
    return jnp.where(lower, -jnp.roll(flat, -half, axis=1), jnp.roll(flat, half, axis=1))


def head_cols(ref, index):
    return ref[:, index * HD : (index + 1) * HD]


def visible_mask(tile, length, ctx_len):
    first = lax.axis_index("ctx") * ctx_len + pl.program_id(0) * tile
    rows = first + lax.broadcasted_iota(jnp.int32, (tile, length), 0)
    return lax.broadcasted_iota(jnp.int32, (tile, length), 1) <= rows


def attend_kernel(ctx_len, q_ref, k_ref, v_ref, o_ref, lse_ref):
    tile, length = q_ref.shape[0], k_ref.shape[0]
    mask = visible_mask(tile, length, ctx_len)
    outs, logs = [], []
    for head in range(HQ):
        group = head // GROUP
        scores = dot_last(head_cols(q_ref, head), head_cols(k_ref, group))
        scores = jnp.where(mask, scores, masked_score)
        top = jnp.max(scores, axis=-1, keepdims=True)
        exps = jnp.exp(scores - top)
        total = jnp.sum(exps, axis=-1, keepdims=True)
        probs = (exps * (1.0 / total)).astype(bf16)
        outs.append(dot(probs, head_cols(v_ref, group)))
        logs.append(top + jnp.log(total))
    o_ref[...] = jnp.concatenate(outs, axis=1).astype(bf16)
    lse_ref[...] = jnp.concatenate(logs + [jnp.zeros((tile, 128 - HQ), f32)], axis=1)


def attend_grad_kernel(ctx_len, q_ref, do_ref, lse_ref, k_ref, v_ref, dq_ref, dk_ref, dv_ref):
    tile, length = q_ref.shape[0], k_ref.shape[0]
    mask = visible_mask(tile, length, ctx_len)

    @pl.when(pl.program_id(0) == 0)
    def _():
        dk_ref[...] = jnp.zeros_like(dk_ref)
        dv_ref[...] = jnp.zeros_like(dv_ref)

    parts = []
    for group in range(KVH):
        keys, values = head_cols(k_ref, group), head_cols(v_ref, group)
        dk = jnp.zeros((HD, length), f32)
        dv = jnp.zeros((HD, length), f32)
        for head in range(group * GROUP, (group + 1) * GROUP):
            query, grad = head_cols(q_ref, head), head_cols(do_ref, head)
            scores = dot_last(query, keys) - lse_ref[:, head : head + 1]
            probs = jnp.exp(jnp.where(mask, scores, masked_score))
            grad_probs = dot_last(grad, values)
            delta = jnp.sum(probs * grad_probs, axis=-1, keepdims=True)
            grad_scores = (probs * (grad_probs - delta)).astype(bf16)
            parts.append(dot(grad_scores, keys) * HD ** (-0.5))
            dk += dot_rows(query, grad_scores)
            dv += dot_rows(grad, probs.astype(bf16))
        dk_ref[group * HD : (group + 1) * HD, :] += dk
        dv_ref[group * HD : (group + 1) * HD, :] += dv
    dq_ref[...] = jnp.concatenate(parts, axis=1)


def rows_spec(tile, width):
    return pl.BlockSpec((tile, width), lambda step: (step, 0))


def whole_spec(rows, width):
    return pl.BlockSpec((rows, width), lambda step: (0, 0))


def attend(queries, keys, values):
    rows, length = queries.shape[0], keys.shape[0]
    tile = min(256, rows)
    return pl.pallas_call(
        functools.partial(attend_kernel, rows),
        grid=(rows // tile,),
        in_specs=[rows_spec(tile, ATT), whole_spec(length, KVH * HD), whole_spec(length, KVH * HD)],
        out_specs=[rows_spec(tile, ATT), rows_spec(tile, 128)],
        out_shape=[
            jax.ShapeDtypeStruct((rows, ATT), bf16),
            jax.ShapeDtypeStruct((rows, 128), f32),
        ],
        compiler_params=pltpu.CompilerParams(vmem_limit_bytes=40 << 20),
        cost_estimate=pl.CostEstimate(
            flops=8 * rows * length * ATT, bytes_accessed=4 << 20, transcendentals=rows * length * HQ
        ),
    )(queries, keys, values)


def attend_grad(queries, grads, lse, keys, values):
    rows, length = queries.shape[0], keys.shape[0]
    tile = min(256, rows)
    pair = whole_spec(length, KVH * HD)
    flipped = whole_spec(KVH * HD, length)
    return pl.pallas_call(
        functools.partial(attend_grad_kernel, rows),
        grid=(rows // tile,),
        in_specs=[rows_spec(tile, ATT), rows_spec(tile, ATT), rows_spec(tile, 128), pair, pair],
        out_specs=[rows_spec(tile, ATT), flipped, flipped],
        out_shape=[
            jax.ShapeDtypeStruct((rows, ATT), f32),
            jax.ShapeDtypeStruct((KVH * HD, length), f32),
            jax.ShapeDtypeStruct((KVH * HD, length), f32),
        ],
        compiler_params=pltpu.CompilerParams(vmem_limit_bytes=40 << 20),
        cost_estimate=pl.CostEstimate(
            flops=24 * rows * length * ATT, bytes_accessed=6 << 20, transcendentals=rows * length * HQ
        ),
    )(queries, grads, lse, keys, values)


def per_device(layer_input, w_qkv, b_qkv, g_attn, w_out, g_mlp, w_gate, w_up, w_down, cotangent):
    sequences, local_len, width = layer_input.shape
    token_rows = sequences * local_len
    half = width // 2
    key_width = KVH * HD
    ctx_size, dp_size = lax.axis_size("ctx"), lax.axis_size("dp")
    group_size = ctx_size * dp_size
    own_index = lax.axis_index("ctx")
    first = lax.axis_index("fsdp") == 0

    def swap(value):
        return partner(value, "fsdp", 0)

    def joined_rows(own, other):
        axis = 0
        return jnp.where(
            first,
            jnp.concatenate([own, other], axis=axis),
            jnp.concatenate([other, own], axis=axis),
        )

    def joined_cols(own, other):
        return jnp.where(
            first, jnp.concatenate([own, other], axis=1), jnp.concatenate([other, own], axis=1)
        )

    def split_cols(value):
        cut = value.shape[1] // 2
        left, right = value[:, :cut], value[:, cut:]
        return jnp.where(first, left, right), jnp.where(first, right, left)

    vector = jnp.concatenate([b_qkv, g_attn, g_mlp])
    full_qkv = joined_rows(w_qkv, swap(w_qkv))
    vector_other = swap(vector)
    full_out = joined_rows(w_out, swap(w_out))
    gate_other, up_other, down_other = swap(w_gate), swap(w_up), swap(w_down)
    bias_len = b_qkv.shape[0]
    full_bias = joined_rows(vector[:bias_len], vector_other[:bias_len]).astype(f32)
    gain_one = joined_rows(
        vector[bias_len : bias_len + half], vector_other[bias_len : bias_len + half]
    ).astype(f32)
    gain_two = joined_rows(vector[bias_len + half :], vector_other[bias_len + half :]).astype(f32)

    inputs = layer_input.reshape(token_rows, width).astype(f32)
    scale_one = lax.rsqrt(jnp.mean(inputs * inputs, axis=-1, keepdims=True) + epsilon)
    normed_one = (inputs * scale_one * gain_one).astype(bf16)
    joined = dot(normed_one, full_qkv) + full_bias
    positions = (own_index * local_len + jnp.arange(local_len, dtype=jnp.int32)).astype(f32)
    cos_table, sin_table = tables(positions, ATT + key_width)
    cos_table = jnp.tile(cos_table, (sequences, 1))
    sin_table = jnp.tile(sin_table, (sequences, 1))
    turned = joined[:, : ATT + key_width]
    turned = (turned * cos_table + swap_halves(turned) * sin_table).astype(bf16)
    queries = (turned[:, :ATT] * HD ** (-0.5)).astype(bf16).reshape(sequences, local_len, ATT)
    own_pair = jnp.concatenate([turned[:, ATT:], joined[:, ATT + key_width :].astype(bf16)], axis=1)
    own_pair = own_pair.reshape(sequences, local_len, 2 * key_width)
    if ctx_size == 2:
        other_pair = partner(own_pair, "ctx", 0)
        pairs = jnp.where(
            own_index == 0,
            jnp.concatenate([own_pair, other_pair], axis=1),
            jnp.concatenate([other_pair, own_pair], axis=1),
        )
    else:
        pairs = lax.all_gather(own_pair, "ctx", axis=1, tiled=True)
    keys, values = pairs[..., :key_width], pairs[..., key_width:]
    mixed = [attend(queries[s], keys[s], values[s]) for s in range(sequences)]
    attended = jnp.concatenate([m[0] for m in mixed], axis=0)
    hidden = inputs + dot(attended, full_out)
    scale_two = lax.rsqrt(jnp.mean(hidden * hidden, axis=-1, keepdims=True) + epsilon)
    normed_two = (hidden * scale_two * gain_two).astype(bf16)
    two_mine, two_other = split_cols(normed_two)
    gate_pre = dot(two_mine, w_gate) + dot(two_other, gate_other)
    up_value = dot(two_mine, w_up) + dot(two_other, up_other)
    gate_sig = jax.nn.sigmoid(gate_pre)
    swish = gate_pre * gate_sig
    product = (swish * up_value).astype(bf16)
    product_mine, product_other = split_cols(product)
    upstream = cotangent.reshape(token_rows, width)

    ctx_order = [("ctx", bit) for bit in range(bits_of("ctx"))]
    near = [("dp", 0)] if dp_size > 1 else []
    far = [("dp", bit) for bit in range(1, bits_of("dp"))]
    order_a = ctx_order + near + far
    order_b = near + ctx_order + far

    down_sent = swap(dot_rows(upstream, product_other).astype(bf16))
    down_sum = (dot_rows(upstream, product_mine) + down_sent.astype(f32)).astype(bf16)
    down_sum = down_sum.reshape(group_size, width // group_size, -1)
    cut = (down_sum.shape[2] // 256) * 128
    downs = [Halving(down_sum[..., :cut], order_a), Halving(down_sum[..., cut:], order_b)]

    product_grads = after(
        (dot_last(upstream, w_down), dot_last(upstream, down_other), product_mine, product_other),
        downs,
    )
    step_all(downs)
    grad_product = joined_cols(product_grads[0], product_grads[1])
    activations = hidden + (dot(product_grads[2], w_down) + dot(product_grads[3], down_other))
    grad_gate = (grad_product * up_value * gate_sig * (1.0 + gate_pre * (1.0 - gate_sig))).astype(
        bf16
    )
    grad_up = (grad_product * swish).astype(bf16)

    def weight_sums(grad):
        sent = swap(dot_rows(grad, two_other).astype(bf16))
        total = (dot_rows(grad, two_mine) + sent.astype(f32)).astype(bf16)
        total = total.reshape(group_size, -1, half)
        cut = total.shape[1] // 16 * 8
        return [Halving(total[:, :cut], order_a), Halving(total[:, cut:], order_b)]

    gates, ups = weight_sums(grad_gate), weight_sums(grad_up)
    grad_gate, grad_up = after((grad_gate, grad_up), downs + gates + ups)
    step_all(downs + gates)

    grad_normed_two = joined_cols(
        dot_last(grad_gate, w_gate) + dot_last(grad_up, w_up),
        dot_last(grad_gate, gate_other) + dot_last(grad_up, up_other),
    )
    gain_two_grad = jnp.sum(grad_normed_two * hidden * scale_two, axis=0)
    scaled_two = grad_normed_two * gain_two
    grad_hidden = (
        upstream.astype(f32)
        + scale_two * scaled_two
        - hidden * scale_two**3 * jnp.mean(scaled_two * hidden, axis=-1, keepdims=True)
    )
    grad_hidden, grad_hidden_low = after((grad_hidden, grad_hidden.astype(bf16)), downs + gates)
    step_all(downs + gates + ups)
    out_grad = dot_last(grad_hidden_low, full_out).astype(bf16).reshape(sequences, local_len, ATT)
    grads = [
        attend_grad(queries[s], out_grad[s], mixed[s][1], keys[s], values[s])
        for s in range(sequences)
    ]
    grad_q = jnp.concatenate([g[0] for g in grads], axis=0)
    grad_pairs = jnp.stack([jnp.concatenate([g[1], g[2]], axis=0).T for g in grads])
    grad_q, grad_pairs = after((grad_q, grad_pairs), downs + gates + ups)
    grad_down = jnp.concatenate([one.finish() for one in downs], axis=1).astype(f32).T
    grad_gate_w = jnp.concatenate([one.finish() for one in gates], axis=0).astype(f32).T
    grad_up_w = jnp.concatenate([one.finish() for one in ups], axis=0).astype(f32).T
    if ctx_size == 2:
        lower, upper = grad_pairs[:, :local_len], grad_pairs[:, local_len:]
        sent = jnp.where(own_index == 0, upper, lower).astype(bf16)
        grad_pair = jnp.where(own_index == 0, lower, upper) + partner(sent, "ctx", 0).astype(f32)
    else:
        grad_pair = lax.psum_scatter(
            grad_pairs.astype(bf16), "ctx", scatter_dimension=1, tiled=True
        ).astype(f32)
    grad_pair = grad_pair.reshape(token_rows, 2 * key_width)
    grad_turned = jnp.concatenate([grad_q, grad_pair[:, :key_width]], axis=1)
    grad_turned = grad_turned * cos_table - swap_halves(grad_turned * sin_table)
    grad_joined = jnp.concatenate([grad_turned, grad_pair[:, key_width:]], axis=1).astype(bf16)

    att_mine, att_other = split_cols(attended)
    one_mine, one_other = split_cols(normed_one)

    def by_group(qkv_part, out_part):
        return jnp.concatenate(
            [
                qkv_part.reshape(group_size, -1, half),
                out_part.reshape(group_size, -1, half),
            ],
            axis=1,
        )

    small_sent = swap(
        by_group(dot_rows(grad_joined, one_other), dot_rows(grad_hidden_low, att_other)).astype(bf16)
    )
    small = by_group(dot_rows(grad_joined, one_mine), dot_rows(grad_hidden_low, att_mine))
    small = (small + small_sent.astype(f32)).astype(bf16)
    small = Halving(small, order_a).finish().astype(f32)
    qkv_rows = QKV // group_size
    grad_qkv_w, grad_out_w = small[:qkv_rows].T, small[qkv_rows:].T

    grad_bias = jnp.sum(grad_joined.astype(f32), axis=0)
    grad_normed_one = dot_last(grad_joined, full_qkv)
    gain_one_grad = jnp.sum(grad_normed_one * inputs * scale_one, axis=0)
    scaled_one = grad_normed_one * gain_one
    grad_input = (
        grad_hidden
        + scale_one * scaled_one
        - inputs * scale_one**3 * jnp.mean(scaled_one * inputs, axis=-1, keepdims=True)
    )
    packed = sum_everywhere(jnp.concatenate([grad_bias, gain_one_grad, gain_two_grad])[None])[0]

    def own_half(begin, length):
        part = packed[begin : begin + length]
        return jnp.where(first, part[: length // 2], part[length // 2 :])

    return (
        activations.reshape(sequences, local_len, width),
        grad_input.reshape(sequences, local_len, width),
        grad_qkv_w,
        own_half(0, QKV),
        own_half(QKV, width),
        grad_out_w,
        own_half(QKV + width, width),
        grad_gate_w,
        grad_up_w,
        grad_down,
    )


def solution(mesh):
    in_specs = (
        P(("dp", "fsdp"), "ctx", None),
        P("fsdp", None),
        P("fsdp"),
        P("fsdp"),
        P("fsdp", None),
        P("fsdp"),
        P("fsdp", None),
        P("fsdp", None),
        P("fsdp", None),
        P(("dp", "fsdp"), "ctx", None),
    )
    out_specs = (
        P(("dp", "fsdp"), "ctx", None),
        P(("dp", "fsdp"), "ctx", None),
        P("fsdp", ("dp", "ctx")),
        P("fsdp"),
        P("fsdp"),
        P("fsdp", ("dp", "ctx")),
        P("fsdp"),
        P("fsdp", ("dp", "ctx")),
        P("fsdp", ("dp", "ctx")),
        P("fsdp", ("dp", "ctx")),
    )
    return jax.shard_map(
        per_device, mesh=mesh, in_specs=in_specs, out_specs=out_specs, check_vma=False
    )
```
